32 devices in a mesh: shard: 2 (over x), ex: 8 (over z, y), tp: 2 (over core).
Axes of the slice: x: 2, y: 2, z: 4, core: 2. Of those that a mesh axis runs over, the one named last changes fastest.
Arguments:
- hidden: bfloat16 [4096, 28672], P(('shard', 'ex'), 'tp'), parts along dimension 0, may hold values from -6 to 6
- out_grad: bfloat16 [4096, 8192], P(('shard', 'ex'), 'tp'), parts along dimension 0, may hold values from -6 to 6
- token_live: int32 [4096], P(('shard', 'ex')), parts along dimension 0, may hold values 0 or 1
- proj_in: bfloat16 [28672, 64], P('tp'), may hold values from -0.03125 to 0.03125
- proj_out: bfloat16 [8192, 64], P('tp'), may hold values from -0.0625 to 0.0625
- query_bank: bfloat16 [1024, 4096], P('ex'), may hold values from -0.01171875 to 0.01171875
Outputs:
- scores: float32 [64, 1024], P(('shard', 'ex')), parts along dimension 0
The draws below stay inside these ranges and needn't reach their ends.
There are 2 independent parts, one for each index of `shard`. The reference program is written for one: setup_inputs(seed, part) draws one part's arguments, and reference() takes and returns one part's arrays. A program takes and returns all parts, laid end to end along the dimension named above; an argument that names none is the same for every part. Nothing has to cross between parts.
All inputs are finite; a program needn't handle non-finite values. No bound on the sum of `token_live` on one device may be relied on, other than what follows from the above.
Results may differ from the reference program's by a relative error of at most 0.0029.
Values may be sent and summed in bfloat16 or wider, within the bound.
A program may use at most 64 MiB of HBM per device.

```python
import jax
import jax.numpy as jnp
from jax import lax

D = 8192
FF = 28672
R1 = 64
R2 = 64
QUERIES = 1024
SEQ = 64
EXAMPLES = 32
TOKENS = 2048


def place_ends(drawn, rng, low, top_value):
    shape = drawn.shape
    index_at = [jax.random.randint(jax.random.fold_in(rng, axis), (), 0, shape[axis]) for axis in range(len(shape))]
    drawn = drawn.at[tuple(index_at)].set(low)
    longest = shape.index(max(shape))
    index_at[longest] = (index_at[longest] + 1) % shape[longest]
    return drawn.at[tuple(index_at)].set(top_value)


def block_levels(stream_key, extent, pieces, smallest, largest):
    def one(axis_at, blocks):
        steps = jax.random.uniform(jax.random.fold_in(jax.random.fold_in(stream_key, 6), axis_at), (blocks,), jnp.float32, smallest / len(pieces), largest / len(pieces))
        return jnp.repeat(jnp.exp(steps), extent[axis_at] // blocks).reshape((-1,) + (1,) * (len(extent) - axis_at - 1))

    level = one(*pieces[0])
    for cut in pieces[1:]:
        level = level * one(*cut)
    return level


def centred(rng, dims, scale, limit, cuts=(), kind=jnp.bfloat16):
    result = scale * jax.random.normal(rng, dims, jnp.float32)
    if cuts:
        result = result * block_levels(rng, dims, cuts, -0.22, 0.18)
    return jnp.clip(result, -limit, limit).astype(kind)


def setup_inputs(seed: int = 0, part: int = 0) -> dict:
    arg_keys = jax.random.split(jax.random.key(seed), 7)
    part_splits = jax.random.split(jax.random.fold_in(arg_keys[6], part), 7)
    return {
        "hidden": centred(part_splits[0], (TOKENS, FF), 1.0, 6.0, ((0, 8), (1, 2))),
        "out_grad": centred(part_splits[1], (TOKENS, D), 1.0, 6.0, ((0, 8), (1, 2))),
        "token_live": place_ends((jax.random.randint(part_splits[2], (TOKENS,), 0, 4) < 3).astype(jnp.int32), jax.random.fold_in(part_splits[2], 1), 0, 1),
        "proj_in": centred(arg_keys[3], (FF, R1), FF ** -0.5, 0.03125, ((0, 2),)),
        "proj_out": centred(arg_keys[4], (D, R2), D ** -0.5, 0.0625, ((0, 2),)),
        "query_bank": centred(arg_keys[5], (QUERIES, R1 * R2), (R1 * R2 * SEQ) ** -0.5, 0.01171875, ((0, 8),)),
    }


def reference(hidden, out_grad, token_live, proj_in, proj_out, query_bank):
    live = token_live.astype(jnp.float32)[:, None]
    in_proj = jnp.dot(hidden, proj_in, preferred_element_type=jnp.float32) * live
    out_proj = jnp.dot(out_grad, proj_out, preferred_element_type=jnp.float32)
    left = in_proj.reshape(EXAMPLES, SEQ, R1)
    right = out_proj.reshape(EXAMPLES, SEQ, R2)
    grads = jnp.einsum("eti,etj->eij", left, right, precision=lax.Precision.HIGHEST)
    grads = grads.reshape(EXAMPLES, R1 * R2).astype(jnp.bfloat16)
    return jnp.dot(grads, query_bank.T, preferred_element_type=jnp.float32)
```

```python
import functools

import jax
import jax.numpy as jnp
from jax import lax
from jax.experimental import pallas as pl
from jax.experimental.pallas import tpu as pltpu
from jax.sharding import PartitionSpec as P

R1 = 64
R2 = 64
SEQ = 64
LANES = 128
CHUNKS = 4
MESH = pl.DeviceIdType.MESH
NT = (((1,), (1,)), ((), ()))


def each(n, body):
    if n <= 16:
        for i in range(n):
            body(i)
    else:
        lax.fori_loop(0, n, lambda i, _: (body(i), 0)[1], 0)


def kernel(
    n_ex, hid_hbm, og_hbm, live_hbm, pin_hbm, pout_hbm, qb_hbm, res_hbm,
    hid, og, live, pin, pout, qb, msg_out, msg_in, in_t, grads, wide, sbuf,
    hid_sem, pin_sem, og_sem, small_sem, tp_sem, g_send, g_recv, s_send, s_recv, own_sem,
):
    shard, ex, tp = lax.axis_index("shard"), lax.axis_index("ex"), lax.axis_index("tp")
    half = hid_hbm.shape[0] // 2
    own_ex = half // SEQ
    block = own_ex * R1 * R2 // LANES
    pairs = R1 * R2 // LANES
    rows = (pl.ds(pl.multiple_of((1 - tp) * half, half), half), pl.ds(pl.multiple_of(tp * half, half), half))
    width = hid_hbm.shape[1] // CHUNKS

    loads = {}

    def load(name, src, dst, sem):
        loads[name] = pltpu.make_async_copy(src, dst, sem)
        loads[name].start()

    load("pout", pout_hbm, pout, small_sem.at[0])
    load(("og", 0), og_hbm.at[rows[0]], og.at[0], og_sem.at[0])
    for c in range(CHUNKS):
        cols = pl.ds(c * width, width)
        load(("pin", c), pin_hbm.at[:, cols], pin.at[:, cols], pin_sem.at[c])
        load(("hid", 0, c), hid_hbm.at[rows[0], cols], hid.at[0, :, cols], hid_sem.at[0, c])
    load(("og", 1), og_hbm.at[rows[1]], og.at[1], og_sem.at[1])
    load("live", live_hbm.at[:, rows[1]], live, small_sem.at[1])
    for c in range(CHUNKS):
        cols = pl.ds(c * width, width)
        load(("hid", 1, c), hid_hbm.at[rows[1], cols], hid.at[1, :, cols], hid_sem.at[1, c])
    load("qb", qb_hbm, qb, small_sem.at[2])

    barrier = pltpu.get_barrier_semaphore()

    def greet(s):
        pl.semaphore_signal(
            barrier, inc=1, device_id=(shard, lax.rem(ex + s // 2, n_ex), lax.rem(tp + s % 2, 2)), device_id_type=MESH
        )

    each(2 * n_ex - 1, lambda s: greet(s + 1))

    def project(h):
        loads["og", h].wait()
        if h == 0:
            loads["pout"].wait()
        right = lax.dot_general(og[h], pout[...], NT, preferred_element_type=jnp.float32)
        left = jnp.zeros((half, R1), jnp.float32)
        for c in range(CHUNKS):
            cols = pl.ds(c * width, width)
            if h == 0:
                loads["pin", c].wait()
            loads["hid", h, c].wait()
            left += lax.dot_general(hid[h, :, cols], pin[:, cols], NT, preferred_element_type=jnp.float32)
        return jnp.concatenate([left, right], axis=1)

    msg_out[...] = project(0)
    pl.semaphore_wait(barrier, 2 * n_ex - 1)
    swap = pltpu.make_async_remote_copy(
        src_ref=msg_out, dst_ref=msg_in, send_sem=tp_sem.at[0], recv_sem=tp_sem.at[1],
        device_id=(shard, ex, 1 - tp), device_id_type=MESH,
    )
    swap.start()
    mine = project(1)
    swap.wait_recv()
    both = mine + msg_in[...]

    in_t[...] = both.T[:R1]
    even = in_t[pl.ds(0, R1 // 2, stride=2), :]
    odd = in_t[pl.ds(1, R1 // 2, stride=2), :]
    loads["live"].wait()
    alive = live[...].astype(jnp.float32)
    token = lax.broadcasted_iota(jnp.int32, (1, half), 1)
    lefts = []
    for e in range(own_ex):
        keep = jnp.where((token >= e * SEQ) & (token < (e + 1) * SEQ), alive, 0.0)
        lefts.append(jnp.concatenate([even * keep, odd * keep], axis=1))
    low = lax.broadcasted_iota(jnp.int32, (half, LANES), 1) < R2
    turned = pltpu.roll(both, R2, 1)
    right = jnp.concatenate([jnp.where(low, turned, 0.0), jnp.where(low, 0.0, both)], axis=0)
    grad = jnp.dot(
        jnp.concatenate(lefts, axis=0), right, precision=lax.Precision.HIGHEST, preferred_element_type=jnp.float32
    )
    slot = grads.at[pl.ds(pl.multiple_of(ex * block, block), block)]
    slot[...] = grad.astype(jnp.bfloat16)

    def grad_copy(peer, owner):
        where = grads.at[pl.ds(pl.multiple_of(owner * block, block), block)]
        return pltpu.make_async_remote_copy(
            src_ref=where, dst_ref=where, send_sem=g_send.at[peer], recv_sem=g_recv.at[owner],
            device_id=(shard, peer, tp), device_id_type=MESH,
        )

    def around(s):
        return lax.rem(ex + s, n_ex)

    each(n_ex - 1, lambda s: grad_copy(around(s + 1), ex).start())
    each(n_ex - 1, lambda s: grad_copy(around(s + 1), around(s + 1)).wait_recv())

    wide[...] = grads[...].astype(jnp.float32)
    flat = jnp.concatenate(
        [wide[pl.ds(k, n_ex * own_ex, stride=pairs), :].astype(jnp.bfloat16) for k in range(pairs)], axis=1
    )
    loads["qb"].wait()
    scores = lax.dot_general(flat, qb[...], NT, preferred_element_type=jnp.float32)
    for j in range(n_ex):
        sbuf[j] = scores[j * own_ex : (j + 1) * own_ex]

    def score_copy(peer, core, owner, owner_core):
        return pltpu.make_async_remote_copy(
            src_ref=sbuf.at[peer], dst_ref=res_hbm.at[owner, owner_core],
            send_sem=s_send.at[core, peer], recv_sem=s_recv.at[owner_core, owner],
            device_id=(shard, peer, core), device_id_type=MESH,
        )

    def partner(s):
        return around(s // 2), lax.rem(tp + s % 2, 2)

    each(2 * n_ex - 1, lambda s: score_copy(*partner(s + 1), ex, tp).start())
    keep_own = pltpu.make_async_copy(sbuf.at[ex], res_hbm.at[ex, tp], own_sem)
    keep_own.start()
    swap.wait_send()
    each(n_ex - 1, lambda s: grad_copy(around(s + 1), ex).wait_send())
    each(2 * n_ex - 1, lambda s: score_copy(*partner(s + 1), *partner(s + 1)).wait_recv())
    each(2 * n_ex - 1, lambda s: score_copy(*partner(s + 1), ex, tp).wait_send())
    keep_own.wait()


def local(n_ex, hidden, out_grad, token_live, proj_in, proj_out, query_bank):
    tokens, hid_width = hidden.shape
    half, own_ex = tokens // 2, tokens // 2 // SEQ
    queries = query_bank.shape[0]
    block = own_ex * R1 * R2 // LANES
    hbm = pl.BlockSpec(memory_space=pl.ANY)
    dma = pltpu.SemaphoreType.DMA
    result = pl.pallas_call(
        functools.partial(kernel, n_ex),
        out_shape=jax.ShapeDtypeStruct((n_ex, 2, own_ex, queries), jnp.float32),
        in_specs=[hbm] * 6,
        out_specs=hbm,
        scratch_shapes=[
            pltpu.VMEM((2, half, hid_width), jnp.bfloat16),
            pltpu.VMEM((2, half, out_grad.shape[1]), jnp.bfloat16),
            pltpu.VMEM((1, half), jnp.int32),
            pltpu.VMEM((R1, hid_width), jnp.bfloat16),
            pltpu.VMEM((R2, out_grad.shape[1]), jnp.bfloat16),
            pltpu.VMEM(query_bank.shape, jnp.bfloat16),
            pltpu.VMEM((half, R1 + R2), jnp.float32),
            pltpu.VMEM((half, R1 + R2), jnp.float32),
            pltpu.VMEM((R1, half), jnp.float32),
            pltpu.VMEM((n_ex * block, LANES), jnp.bfloat16),
            pltpu.VMEM((n_ex * block, LANES), jnp.float32),
            pltpu.VMEM((n_ex, own_ex, queries), jnp.float32),
            dma((2, CHUNKS)), dma((CHUNKS,)), dma((2,)), dma((3,)), dma((2,)),
            dma((n_ex,)), dma((n_ex,)), dma((2, n_ex)), dma((2, n_ex)), dma,
        ],
        compiler_params=pltpu.CompilerParams(
            collective_id=0, has_side_effects=True, vmem_limit_bytes=56 * 1024 * 1024
        ),
        name="attribute",
    )(hidden, out_grad, token_live.reshape(1, tokens), proj_in.T, proj_out.T, query_bank)
    return result.reshape(n_ex, 2 * own_ex, queries).transpose(1, 0, 2).reshape(2 * own_ex, n_ex * queries)


def solution(mesh):
    placed = (
        P(("shard", "ex"), "tp"),
        P(("shard", "ex"), "tp"),
        P(("shard", "ex")),
        P("tp", None),
        P("tp", None),
        P("ex", None),
    )
    return jax.shard_map(
        functools.partial(local, mesh.shape["ex"]),
        mesh=mesh, in_specs=placed, out_specs=P(("shard", "ex"), None), check_vma=False,
    )
```

```python
import functools

import jax
import jax.numpy as jnp
from jax import lax
from jax.experimental import pallas as pl
from jax.experimental.pallas import tpu as pltpu
from jax.sharding import PartitionSpec as P

R1 = 64
R2 = 64
SEQ = 64
LANES = 128
MESH = pl.DeviceIdType.MESH
NT = (((1,), (1,)), ((), ()))


def each(n, body):
    if n <= 16:
        for i in range(n):
            body(i)
    else:
        lax.fori_loop(0, n, lambda i, _: (body(i), 0)[1], 0)


def kernel(
    n_ex, hid_hbm, og_hbm, live_hbm, pin_hbm, pout_hbm, qb_hbm, res,
    hid, og, live, pin, pout, qb, msg_out, msg_in, in_t, grads, wide, sbuf,
    hid_sem, og_sem, small_sem, tp_sem, g_send, g_recv, s_send, s_recv,
):
    shard, ex, tp = lax.axis_index("shard"), lax.axis_index("ex"), lax.axis_index("tp")
    half = hid_hbm.shape[0] // 2
    own_ex = half // SEQ
    pairs = R1 * R2 // LANES
    theirs, ours = pl.multiple_of((1 - tp) * half, half), pl.multiple_of(tp * half, half)

    def load(src, dst, sem):
        copy = pltpu.make_async_copy(src, dst, sem)
        copy.start()
        return copy

    get_pout = load(pout_hbm, pout, small_sem.at[0])
    get_og = [load(og_hbm.at[pl.ds(theirs, half)], og.at[pl.ds(0, half)], og_sem.at[0])]
    get_pin = load(pin_hbm, pin, small_sem.at[1])
    get_first = load(hid_hbm.at[pl.ds(theirs, half)], hid.at[pl.ds(0, half)], hid_sem.at[0])
    get_og.append(load(og_hbm.at[pl.ds(ours, half)], og.at[pl.ds(half, half)], og_sem.at[1]))
    get_live = load(live_hbm.at[:, pl.ds(ours, half)], live, small_sem.at[2])
    get_second = load(hid_hbm.at[pl.ds(ours, half)], hid.at[pl.ds(half, half)], hid_sem.at[1])
    get_qb = load(qb_hbm, qb, small_sem.at[3])

    def around(s):
        return jnp.where(ex + s >= n_ex, ex + s - n_ex, ex + s)

    def partner(s):
        return around(s // 2), (tp if s % 2 == 0 else 1 - tp) if isinstance(s, int) else lax.rem(tp + s % 2, 2)

    barrier = pltpu.get_barrier_semaphore()

    def greet(s):
        pl.semaphore_signal(barrier, inc=1, device_id=(shard, *partner(s)), device_id_type=MESH)

    each(2 * n_ex - 1, lambda s: greet(s + 1))

    get_pout.wait()
    get_og[0].wait()
    msg_out[R1:] = lax.dot_general(pout[...], og[:half], NT, preferred_element_type=jnp.float32)
    get_pin.wait()
    get_first.wait()
    msg_out[:R1] = lax.dot_general(pin[...], hid[:half], NT, preferred_element_type=jnp.float32)
    pl.semaphore_wait(barrier, 2 * n_ex - 1)
    swap = pltpu.make_async_remote_copy(
        src_ref=msg_out, dst_ref=msg_in, send_sem=tp_sem.at[0], recv_sem=tp_sem.at[1],
        device_id=(shard, ex, 1 - tp), device_id_type=MESH,
    )
    swap.start()

    def grad_copy(peer, owner):
        block = own_ex * pairs
        where = grads.at[pl.ds(pl.multiple_of(owner * block, block), block)]
        return pltpu.make_async_remote_copy(
            src_ref=where, dst_ref=where, send_sem=g_send.at[peer], recv_sem=g_recv.at[owner],
            device_id=(shard, peer, tp), device_id_type=MESH,
        )

    get_og[1].wait()
    right = lax.dot_general(pout[...], og[half:], NT, preferred_element_type=jnp.float32)
    get_live.wait()
    get_second.wait()
    left = lax.dot_general(pin[...], hid[half:], NT, preferred_element_type=jnp.float32)
    swap.wait_recv()
    in_half = (left + msg_in[:R1]) * live[...].astype(jnp.float32)
    out_t = right + msg_in[R1:]

    in_t[...] = in_half
    even = in_t[pl.ds(0, R1 // 2, stride=2), :]
    odd = in_t[pl.ds(1, R1 // 2, stride=2), :]
    token = lax.broadcasted_iota(jnp.int32, (1, half), 1)
    lefts = []
    for e in range(own_ex):
        mine = (token >= e * SEQ) & (token < (e + 1) * SEQ)
        lefts.append(jnp.concatenate([jnp.where(mine, even, 0.0), jnp.where(mine, odd, 0.0)], axis=1))
    none = jnp.zeros_like(out_t)
    both = jnp.concatenate(
        [jnp.concatenate([out_t, none], axis=1), jnp.concatenate([none, out_t], axis=1)], axis=0
    )
    grad = lax.dot_general(
        jnp.concatenate(lefts, axis=0), both, NT,
        precision=lax.Precision.HIGHEST, preferred_element_type=jnp.float32,
    )
    block = own_ex * pairs
    grads[pl.ds(pl.multiple_of(ex * block, block), block)] = grad.astype(jnp.bfloat16)
    each(n_ex - 1, lambda s: grad_copy(around(s + 1), ex).start())
    each(n_ex - 1, lambda s: grad_copy(around(s + 1), around(s + 1)).wait_recv())

    wide[...] = grads[...].astype(jnp.float32)
    flat = jnp.concatenate(
        [wide[pl.ds(k, n_ex * own_ex, stride=pairs), :].astype(jnp.bfloat16) for k in range(pairs)], axis=1
    )
    get_qb.wait()
    scores = lax.dot_general(flat, qb[...], NT, preferred_element_type=jnp.float32)
    for j in range(n_ex):
        sbuf[j] = scores[j * own_ex : (j + 1) * own_ex]

    def score_copy(peer, core, owner, owner_core):
        return pltpu.make_async_remote_copy(
            src_ref=sbuf.at[peer], dst_ref=res.at[owner, owner_core],
            send_sem=s_send.at[core, peer], recv_sem=s_recv.at[owner_core, owner],
            device_id=(shard, peer, core), device_id_type=MESH,
        )

    each(2 * n_ex - 1, lambda s: score_copy(*partner(s + 1), ex, tp).start())
    res[ex, tp] = sbuf[ex]
    swap.wait_send()
    each(n_ex - 1, lambda s: grad_copy(around(s + 1), ex).wait_send())
    each(2 * n_ex - 1, lambda s: score_copy(*partner(s + 1), *partner(s + 1)).wait_recv())
    each(2 * n_ex - 1, lambda s: score_copy(*partner(s + 1), ex, tp).wait_send())


def local(n_ex, hidden, out_grad, token_live, proj_in, proj_out, query_bank):
    tokens, hid_width = hidden.shape
    half, own_ex = tokens // 2, tokens // 2 // SEQ
    queries = query_bank.shape[0]
    block = own_ex * R1 * R2 // LANES
    hbm = pl.BlockSpec(memory_space=pl.ANY)
    dma = pltpu.SemaphoreType.DMA
    result = pl.pallas_call(
        functools.partial(kernel, n_ex),
        out_shape=pltpu.VMEM((n_ex, 2, own_ex, queries), jnp.float32),
        in_specs=[hbm] * 6,
        out_specs=pl.BlockSpec(memory_space=pltpu.VMEM),
        scratch_shapes=[
            pltpu.VMEM((tokens, hid_width), jnp.bfloat16),
            pltpu.VMEM(out_grad.shape, jnp.bfloat16),
            pltpu.VMEM((1, half), jnp.int32),
            pltpu.VMEM((R1, hid_width), jnp.bfloat16),
            pltpu.VMEM((R2, out_grad.shape[1]), jnp.bfloat16),
            pltpu.VMEM(query_bank.shape, jnp.bfloat16),
            pltpu.VMEM((R1 + R2, half), jnp.float32),
            pltpu.VMEM((R1 + R2, half), jnp.float32),
            pltpu.VMEM((R1, half), jnp.float32),
            pltpu.VMEM((n_ex * block, LANES), jnp.bfloat16),
            pltpu.VMEM((n_ex * block, LANES), jnp.float32),
            pltpu.VMEM((n_ex, own_ex, queries), jnp.float32),
            dma((2,)), dma((2,)), dma((4,)), dma((2,)),
            dma((n_ex,)), dma((n_ex,)), dma((2, n_ex)), dma((2, n_ex)),
        ],
        compiler_params=pltpu.CompilerParams(
            collective_id=0, has_side_effects=True, vmem_limit_bytes=56 * 1024 * 1024
        ),
        name="attribute",
    )(hidden, out_grad, token_live.reshape(1, tokens), proj_in.T, proj_out.T, query_bank)
    return result.reshape(n_ex, 2 * own_ex, queries).transpose(1, 0, 2).reshape(2 * own_ex, n_ex * queries)


def solution(mesh):
    placed = (
        P(("shard", "ex"), "tp"),
        P(("shard", "ex"), "tp"),
        P(("shard", "ex")),
        P("tp", None),
        P("tp", None),
        P("ex", None),
    )
    return jax.shard_map(
        functools.partial(local, mesh.shape["ex"]),
        mesh=mesh, in_specs=placed, out_specs=P(("shard", "ex"), None), check_vma=False,
    )
```
